128 devices in a mesh: row: 16 (over z_hi, x, core), col: 8 (over z_lo, y).
Axes of the slice: x: 4, y: 4, z: 4 (z_hi: 2, z_lo: 2; z = z_hi * 2 + z_lo), core: 2. Of those that a mesh axis runs over, the one named last changes fastest.
Arguments:
- momentum: bfloat16 [6144, 8192], P('row', 'col'), may hold values from -0.029831067 to 0.029831067
Outputs:
- update: bfloat16 [6144, 8192], P('row', 'col')
The draws below stay inside these ranges and needn't reach their ends.
All inputs are finite; a program needn't handle non-finite values.
Results may differ from the reference program's by a relative error of at most 0.0035.
Values may be sent and summed in bfloat16 or wider, within the bound.
A program may use at most 128 MiB of HBM per device.

```python
import math
import jax
import jax.numpy as jnp

M = 6144
N = 8192


def draw_momentum(key, part):
    key = jax.random.fold_in(key, 11)
    noise_key = jax.random.fold_in(key, 0)
    base = 0.45 / math.sqrt(N)
    bound = 2.7 / math.sqrt(N)
    values = base * jax.random.normal(noise_key, (M, N), jnp.float32)
    return jnp.clip(values, -bound, bound).astype(jnp.bfloat16)


def setup_inputs(seed: int = 0) -> dict:
    key_list = jax.random.split(jax.random.key(seed), 2)
    momentum = draw_momentum(jax.random.fold_in(key_list[1], 71), 0)
    return dict(momentum=momentum)


def reference(momentum):
    gram = jnp.dot(momentum, momentum.T, preferred_element_type=jnp.float32).astype(jnp.bfloat16)
    square = jnp.dot(gram, gram, preferred_element_type=jnp.float32)
    mixed = (-4.775 * gram.astype(jnp.float32) + 2.0315 * square).astype(jnp.bfloat16)
    result = 3.4445 * momentum.astype(jnp.float32) + jnp.dot(mixed, momentum, preferred_element_type=jnp.float32)
    factor = 0.2 * math.sqrt(max(M, N))
    return (factor * result).astype(jnp.bfloat16)
```

```python
import functools
import math

import jax
import jax.numpy as jnp
from jax import lax
from jax.experimental import pallas as pl
from jax.experimental.pallas import tpu as pltpu
from jax.sharding import PartitionSpec as P

M = 6144
N = 8192
MESH = pl.DeviceIdType.MESH
BF = jnp.bfloat16
F32 = jnp.float32

A, B, C = 3.4445, -4.775, 2.0315
FACTOR = 0.2 * math.sqrt(max(M, N))

R = 384
S_ROWS = 2 * R
K = 1024
Q = R // 4
H = Q // 2
N_SITES = 240


def kernel(x_ref, o_ref, xc, wc, pb, g, r1l, r1r, r2l, r2r, zr, ua, local_sem, send_sem, recv_sem):
    row = lax.axis_index("row")
    col = lax.axis_index("col")
    zh, x, core = row // 8, (row % 8) // 2, row % 2
    zl, y = col // 4, col % 4

    xr = {"row": zh * 8 + ((x + 1) % 4) * 2 + core}
    xl = {"row": zh * 8 + ((x + 3) % 4) * 2 + core}
    zp = {"row": (1 - zh) * 8 + x * 2 + core}
    sib = {"row": zh * 8 + x * 2 + (1 - core)}
    yr = {"col": zl * 4 + (y + 1) % 4}
    yl = {"col": zl * 4 + (y + 3) % 4}
    zq = {"col": (1 - zl) * 4 + y}

    def block(dz, dx):
        return ((zh + dz) % 2) * 4 + (x + dx) % 4

    own_copy = pltpu.make_async_copy(x_ref, xc.at[block(0, 0), pl.ds(core * R, R)], local_sem)
    own_copy.start()

    barrier = pltpu.get_barrier_semaphore()
    for peer in (xr, xl, zp, sib, yr, yl, zq):
        pl.semaphore_signal(barrier, inc=1, device_id=peer, device_id_type=MESH)
    pl.semaphore_wait(barrier, 7)

    sites = {}
    pending = []

    def site(name):
        return sites.setdefault(name, len(sites))

    def send(name, src, dst, device):
        i = site(name)
        copy = pltpu.make_async_remote_copy(
            src_ref=src, dst_ref=dst, send_sem=send_sem.at[i], recv_sem=recv_sem.at[i],
            device_id=device, device_id_type=MESH,
        )
        copy.start()
        pending.append(copy)

    def recv(name, view):
        i = site(name)
        pltpu.make_async_remote_copy(
            src_ref=view, dst_ref=view, send_sem=send_sem.at[i], recv_sem=recv_sem.at[i],
            device_id=sib, device_id_type=MESH,
        ).wait_recv()

    def ag(tag, buf, off, n):
        h = n // 2

        def at(dz, dx, o=0, m=n, c=core):
            return buf.at[block(dz, dx), pl.ds(pl.multiple_of(c * R + off + o, 16), m)]

        def to(name, dz, dx, device, o=0, m=n, src=None):
            send(tag + name, at(dz, dx, o, m) if src is None else src, at(dz, dx, o, m), device)

        def own(src=None):
            to("own_r", 0, 0, xr, src=src)
            to("own_l", 0, 0, xl, src=src)
            to("own_z", 0, 0, zp, src=src)
            to("own_s", 0, 0, sib, src=src)

        def near():
            recv(tag + "own_z", at(1, 0))
            to("z_r", 1, 0, xr)
            to("z_l", 1, 0, xl)
            to("z_s", 1, 0, sib)
            recv(tag + "own_r", at(0, -1))
            to("own_rr", 0, -1, xr, 0, h)
            to("l_s", 0, -1, sib)
            recv(tag + "own_l", at(0, 1))
            to("own_ll", 0, 1, xl, h, h)
            to("r_s", 0, 1, sib)

        def mid():
            recv(tag + "z_r", at(1, -1))
            to("z_rr", 1, -1, xr, 0, h)
            to("zl_s", 1, -1, sib)
            recv(tag + "z_l", at(1, 1))
            to("z_ll", 1, 1, xl, h, h)
            to("zr_s", 1, 1, sib)

        def far():
            recv(tag + "own_rr", at(0, 2, 0, h))
            to("f1_s", 0, 2, sib, 0, h)
            recv(tag + "own_ll", at(0, 2, h, h))
            to("f2_s", 0, 2, sib, h, h)

        def last():
            recv(tag + "z_rr", at(1, 2, 0, h))
            to("zf1_s", 1, 2, sib, 0, h)
            recv(tag + "z_ll", at(1, 2, h, h))
            to("zf2_s", 1, 2, sib, h, h)

        def from_sib(dz, dx):
            other = 1 - core
            if dx == 2:
                names = ("zf1_s", "zf2_s") if dz else ("f1_s", "f2_s")
                recv(tag + names[0], at(dz, dx, 0, h, other))
                recv(tag + names[1], at(dz, dx, h, h, other))
                return
            name = {(0, 0): "own_s", (0, -1): "l_s", (0, 1): "r_s", (1, 0): "z_s", (1, -1): "zl_s", (1, 1): "zr_s"}
            recv(tag + name[dz, dx], at(dz, dx, 0, n, other))

        return own, near, mid, far, last, from_sib

    q0, qr, ql, q2 = y * Q, ((y + 1) % 4) * Q, ((y + 3) % 4) * Q, ((y + 2) % 4) * Q

    def rows(off, n):
        return pl.ds(pl.multiple_of(off, 16), n)

    nt = (((1,), (1,)), ((), ()))

    def partial_gram(s):
        for n in range(S_ROWS // 256):
            cols = slice(n * 256, n * 256 + 256)
            p = lax.dot_general(x_ref[...], xc[s, cols, :], nt, preferred_element_type=F32)
            pb[s, :, cols] = p.astype(BF)

    def add(s, off, n, other):
        here = (s, rows(off, n), slice(None))
        pb[here] = (pb[here].astype(F32) + other.astype(F32)).astype(BF)

    def rs1(i, s):
        send(f"rs1r{i}", pb.at[s, rows(q2, H)], r1l.at[s], yr)
        send(f"rs1l{i}", pb.at[s, rows(q2 + H, H)], r1r.at[s], yl)

    def rs2(i, s):
        recv(f"rs1r{i}", r1l.at[s])
        add(s, qr, H, r1l[s])
        send(f"rs2r{i}", pb.at[s, rows(qr, Q)], r2l.at[s], yr)
        recv(f"rs1l{i}", r1r.at[s])
        add(s, ql + H, H, r1r[s])
        send(f"rs2l{i}", pb.at[s, rows(ql, Q)], r2r.at[s], yl)

    def rs3(i, s):
        recv(f"rs2r{i}", r2l.at[s])
        recv(f"rs2l{i}", r2r.at[s])
        add(s, q0, Q, r2l[s].astype(F32) + r2r[s].astype(F32))
        send(f"rs3{i}", pb.at[s, rows(q0, Q)], zr.at[s], zq)

    def rs4(i, s):
        recv(f"rs3{i}", zr.at[s])
        here = (s, rows(q0, Q), slice(None))
        g[here] = (pb[here].astype(F32) + zr[s].astype(F32)).astype(BF)
        send(f"g_r{i}", g.at[s, rows(q0, Q)], g.at[s, rows(q0, Q)], yr)
        send(f"g_l{i}", g.at[s, rows(q0, Q)], g.at[s, rows(q0, Q)], yl)

    def gag(i, s):
        recv(f"g_r{i}", g.at[s, rows(ql, Q)])
        send(f"g_rr{i}", g.at[s, rows(ql, H)], g.at[s, rows(ql, H)], yr)
        recv(f"g_l{i}", g.at[s, rows(qr, Q)])
        send(f"g_ll{i}", g.at[s, rows(qr + H, H)], g.at[s, rows(qr + H, H)], yl)

    def gag_far(i, s):
        recv(f"g_rr{i}", g.at[s, rows(q2, H)])
        recv(f"g_ll{i}", g.at[s, rows(q2 + H, H)])

    own, near, mid, far, last, from_sib = ag("x", xc, 0, R)
    own(x_ref)
    own_copy.wait()

    order = [(0, 0), (1, 0), (0, -1), (0, 1), (1, -1), (1, 1), (0, 2), (1, 2)]
    ids = [block(*d) for d in order]
    stage = [partial_gram, rs1, rs2, rs3, rs4]

    def reduce_steps(i, upto=8):
        if 0 <= i - 1 < 8:
            rs2(i - 1, ids[i - 1])
        if 0 <= i - 2 < 8:
            rs3(i - 2, ids[i - 2])
        if 0 <= i - 3 < 8:
            rs4(i - 3, ids[i - 3])

    events = {1: near, 4: mid, 6: far, 7: last}
    for i, d in enumerate(order):
        if i in events:
            events[i]()
        from_sib(*d)
        partial_gram(ids[i])
        rs1(i, ids[i])
        reduce_steps(i)
    for i in range(8, 11):
        reduce_steps(i)

    def weights(offs):
        for n in range(K // 256):
            cols = slice(n * 256, n * 256 + 256)

            def body(s, acc):
                lhs = [g[s, rows(off, Q), :] for off in offs]
                lhs = lhs[0] if len(lhs) == 1 else jnp.concatenate(lhs, axis=0)
                return acc + jnp.dot(lhs, xc[s, :, cols], preferred_element_type=F32)

            acc = lax.fori_loop(0, 8, body, jnp.zeros((Q * len(offs), 256), F32))
            for j, off in enumerate(offs):
                w = B * x_ref[rows(off, Q), cols].astype(F32) + C * acc[j * Q : (j + 1) * Q]
                wc[block(0, 0), rows(core * R + off, Q), cols] = w.astype(BF)

    quarters = [ag(f"w{j}", wc, off, Q) for j, off in enumerate((q0, ql, qr, q2))]

    weights([q0])
    quarters[0][0]()
    for i in range(8):
        gag(i, ids[i])
    quarters[0][1]()
    weights([ql, qr])
    quarters[1][0]()
    quarters[2][0]()
    quarters[0][2]()
    quarters[0][3]()
    for i in range(8):
        gag_far(i, ids[i])
    weights([q2])
    quarters[3][0]()
    quarters[0][4]()
    for j in (1, 2):
        quarters[j][1]()
    for j in (1, 2):
        quarters[j][2]()
        quarters[j][3]()
    quarters[3][1]()
    for j in (1, 2):
        quarters[j][4]()

    def update(first, s):
        for n in range(K // 256):
            cols = slice(n * 256, n * 256 + 256)
            u = jnp.dot(g[s], wc[s, :, cols], preferred_element_type=F32)
            ua[:, cols] = A * x_ref[:, cols].astype(F32) + u if first else ua[:, cols] + u

    def gathered(d):
        for quarter in quarters:
            quarter[5](*d)

    for i, d in enumerate(order):
        if i == 4:
            quarters[3][2]()
            quarters[3][3]()
        if i == 7:
            quarters[3][4]()
        gathered(d)
        update(i == 0, ids[i])
    o_ref[...] = (FACTOR * ua[...]).astype(BF)

    for copy in pending:
        copy.wait_send()
    assert len(sites) <= N_SITES


def shards(momentum):
    vmem = pl.BlockSpec(memory_space=pltpu.VMEM)
    return pl.pallas_call(
        kernel,
        out_shape=jax.ShapeDtypeStruct((R, K), BF),
        in_specs=[vmem],
        out_specs=vmem,
        scratch_shapes=[
            pltpu.VMEM((8, S_ROWS, K), BF),
            pltpu.VMEM((8, S_ROWS, K), BF),
            pltpu.VMEM((8, R, S_ROWS), BF),
            pltpu.VMEM((8, R, S_ROWS), BF),
            pltpu.VMEM((8, H, S_ROWS), BF),
            pltpu.VMEM((8, H, S_ROWS), BF),
            pltpu.VMEM((8, Q, S_ROWS), BF),
            pltpu.VMEM((8, Q, S_ROWS), BF),
            pltpu.VMEM((8, Q, S_ROWS), BF),
            pltpu.VMEM((R, K), F32),
            pltpu.SemaphoreType.DMA,
            pltpu.SemaphoreType.DMA((N_SITES,)),
            pltpu.SemaphoreType.DMA((N_SITES,)),
        ],
        compiler_params=pltpu.CompilerParams(
            collective_id=0, has_side_effects=True, vmem_limit_bytes=58 << 20
        ),
        cost_estimate=pl.CostEstimate(flops=15 * 10**9, bytes_accessed=2 * R * K * 2, transcendentals=0),
    )(momentum)


def solution(mesh):
    placed = (P("row", "col"),)
    return jax.shard_map(
        shards, mesh=mesh, in_specs=placed, out_specs=P("row", "col"), check_vma=False
    )
```

```python
import functools
import math

import jax
import jax.numpy as jnp
from jax import lax
from jax.experimental import pallas as pl
from jax.experimental.pallas import tpu as pltpu
from jax.sharding import PartitionSpec as P

M = 6144
N = 8192
MESH = pl.DeviceIdType.MESH
BF = jnp.bfloat16
F32 = jnp.float32

A, B, C = 3.4445, -4.775, 2.0315
FACTOR = 0.2 * math.sqrt(max(M, N))

R = 384
S_ROWS = 2 * R
K = 1024
Q = R // 4
H = Q // 2

ORDER = [(0, 0), (0, 3), (0, 1), (1, 0), (0, 2), (1, 2), (1, 3), (1, 1)]
SHAPE = (8, 2, 2, 2, 2, H, K)
HALF = R
N_SEND = 56
N_RECV = 188
CUT = 5


def slot(dz, dx):
    return ORDER.index((dz % 2, dx % 4))


def kernel(x_hbm, o_ref, x_ref, xc, wc, pb, g, r1l, r1r, r2l, r2r, zr, yb, ua, local_sem, send_sem, recv_sem):
    row = lax.axis_index("row")
    col = lax.axis_index("col")
    zh, x, core = row // 8, (row % 8) // 2, row % 2
    zl, y = col // 4, col % 4

    peers = {
        "xr": {"row": zh * 8 + ((x + 1) % 4) * 2 + core},
        "xl": {"row": zh * 8 + ((x + 3) % 4) * 2 + core},
        "zp": {"row": (1 - zh) * 8 + x * 2 + core},
        "sib": {"row": zh * 8 + x * 2 + (1 - core)},
        "yr": {"col": zl * 4 + (y + 1) % 4},
        "yl": {"col": zl * 4 + (y + 3) % 4},
        "zq": {"col": (1 - zl) * 4 + y},
    }

    own_copy = pltpu.make_async_copy(x_hbm, x_ref, local_sem.at[0])
    own_copy.start()
    barrier = pltpu.get_barrier_semaphore()
    for peer in peers.values():
        pl.semaphore_signal(barrier, inc=1, device_id=peer, device_id_type=MESH)
    own_copy.wait()
    places = [
        pltpu.make_async_copy(x_ref.at[pl.ds((c * 4 + i) * H, H)], xc.at[0, c, core, i // 2, i % 2], local_sem.at[1 + c * 4 + i])
        for c in range(2) for i in range(4)
    ]
    for place in places:
        place.start()
    for place in places:
        place.wait()
    pl.semaphore_wait(barrier, len(peers))

    sites = {}
    pending = []

    def site(name):
        return sites.setdefault(name, len(sites))

    def send(name, src, dst, peer):
        i = site(name)
        n = len(pending)
        if n >= N_SEND:
            pending[n - N_SEND].wait_send()
        copy = pltpu.make_async_remote_copy(
            src_ref=src, dst_ref=dst, send_sem=send_sem.at[n % N_SEND], recv_sem=recv_sem.at[i],
            device_id=peers[peer], device_id_type=MESH,
        )
        copy.start()
        pending.append(copy)

    def recv(name, view):
        i = site(name)
        pltpu.make_async_remote_copy(
            src_ref=view, dst_ref=view, send_sem=send_sem.at[0], recv_sem=recv_sem.at[i],
            device_id=peers["sib"], device_id_type=MESH,
        ).wait_recv()

    def rows(off, n):
        return pl.ds(pl.multiple_of(off, 16), n)

    class Gather:
        def __init__(self, tag, buf, index):
            self.tag, self.buf, self.index = tag, buf, index

        def at(self, dz, dx, part=None, c=core):
            view = self.buf.at[(slot(dz, dx), *self.index(c))]
            return view if part is None else view.at[part]

        def to(self, name, dz, dx, peer, part=None):
            there = {"xr": (dz, dx - 1), "xl": (dz, dx + 1), "zp": (1 - dz, dx), "sib": (dz, dx)}[peer]
            send(self.tag + name, self.at(dz, dx, part), self.at(*there, part), peer)

        def recv(self, name, dz, dx, part=None, c=core):
            recv(self.tag + name, self.at(dz, dx, part, c))

        def own(self):
            self.to("own_r", 0, 0, "xr")
            self.to("own_l", 0, 0, "xl")
            self.to("own_z", 0, 0, "zp")
            self.to("own_s", 0, 0, "sib")

        def near(self):
            self.recv("own_r", 0, -1)
            self.to("own_rr", 0, -1, "xr", 0)
            self.to("l_s", 0, -1, "sib")
            self.recv("own_l", 0, 1)
            self.to("own_ll", 0, 1, "xl", 1)
            self.to("r_s", 0, 1, "sib")

        def near_z(self):
            self.recv("own_z", 1, 0)
            self.to("z_s", 1, 0, "sib")

        def pass_z(self):
            self.to("z_r", 1, 0, "xr")
            self.to("z_l", 1, 0, "xl")

        def far(self):
            self.recv("own_rr", 0, 2, 0)
            self.recv("own_ll", 0, 2, 1)
            self.to("f_z", 0, 2, "zp")
            self.to("f_s", 0, 2, "sib")

        def far_z(self):
            self.recv("f_z", 1, 2)
            self.to("zf_s", 1, 2, "sib")

        def mid(self):
            self.recv("z_r", 1, -1)
            self.to("zl_s", 1, -1, "sib")
            self.recv("z_l", 1, 1)
            self.to("zr_s", 1, 1, "sib")

        def from_sib(self, i):
            name = ["own_s", "l_s", "r_s", "z_s", "f_s", "zf_s", "zl_s", "zr_s"][i]
            self.recv(name, *ORDER[i], None, 1 - core)

    q0, qr, ql, q2 = y * Q, ((y + 1) % 4) * Q, ((y + 3) % 4) * Q, ((y + 2) % 4) * Q
    nt = (((1,), (1,)), ((), ()))

    def partial_gram(s, c):
        block = xc[s, c].reshape(HALF, K)
        for m in range(2):
            mine = slice(m * R // 2, (m + 1) * R // 2)
            p = lax.dot_general(x_ref[mine, :], block, nt, preferred_element_type=F32)
            pb[s, c, mine, :] = p.astype(BF)

    def add(s, c, off, n, other):
        here = (s, c, rows(off, n), slice(None))
        pb[here] = (pb[here].astype(F32) + other.astype(F32)).astype(BF)

    def begin(s, c):
        gx[c].from_sib(s)
        partial_gram(s, c)
        send(f"rs1r{s}{c}", pb.at[s, c, rows(q2, H)], r1l.at[s, c], "yr")
        send(f"rs1l{s}{c}", pb.at[s, c, rows(q2 + H, H)], r1r.at[s, c], "yl")

    def rs2(s, c):
        recv(f"rs1r{s}{c}", r1l.at[s, c])
        add(s, c, qr, H, r1l[s, c])
        send(f"rs2r{s}{c}", pb.at[s, c, rows(qr, Q)], r2l.at[s, c], "yr")
        recv(f"rs1l{s}{c}", r1r.at[s, c])
        add(s, c, ql + H, H, r1r[s, c])
        send(f"rs2l{s}{c}", pb.at[s, c, rows(ql, Q)], r2r.at[s, c], "yl")

    def rs3(s, c):
        recv(f"rs2r{s}{c}", r2l.at[s, c])
        recv(f"rs2l{s}{c}", r2r.at[s, c])
        add(s, c, q0, Q, r2l[s, c].astype(F32) + r2r[s, c].astype(F32))
        send(f"rs3{s}{c}", pb.at[s, c, rows(q0, Q)], zr.at[s, c], "zq")

    def rs4(s, c):
        recv(f"rs3{s}{c}", zr.at[s, c])
        total = pb[s, c, rows(q0, Q), :].astype(F32) + zr[s, c].astype(F32)
        g[s, rows(q0, Q), c * HALF : (c + 1) * HALF] = total.astype(BF)

    class GatherGram:
        def __init__(self, s0, s1):
            self.s0, self.s1 = s0, s1

        def at(self, off, t):
            return g.at[self.s0 : self.s1, rows(off + t * H, H)]

        def own(self, t):
            send(f"g_r{self.s0}{t}", self.at(q0, t), self.at(q0, t), "yr")
            send(f"g_l{self.s0}{t}", self.at(q0, t), self.at(q0, t), "yl")

        def near(self, t):
            recv(f"g_r{self.s0}{t}", self.at(ql, t))
            recv(f"g_l{self.s0}{t}", self.at(qr, t))
            if t == 0:
                send(f"g_rr{self.s0}", self.at(ql, 0), self.at(ql, 0), "yr")
            else:
                send(f"g_ll{self.s0}", self.at(qr, 1), self.at(qr, 1), "yl")

        def far(self):
            recv(f"g_rr{self.s0}", self.at(q2, 0))
            recv(f"g_ll{self.s0}", self.at(q2, 1))

    def product(offs, places, s0, s1):
        for n in range(K // 256):
            cols = slice(n * 256, n * 256 + 256)
            part = None
            for s in range(s0, s1):
                lhs = jnp.concatenate([g[s, rows(off, H), :] for off in offs], axis=0)
                rhs = xc[s, :, :, :, :, :, cols].reshape(S_ROWS, 256)
                d = jnp.dot(lhs, rhs, preferred_element_type=F32)
                part = d if part is None else part + d
            for j, (off, place) in enumerate(zip(offs, places)):
                p = part[j * H : (j + 1) * H]
                if s0 > 0:
                    p += yb[rows(off, H), cols]
                if s1 < 8:
                    yb[rows(off, H), cols] = p
                else:
                    w = B * x_ref[rows(off, H), cols].astype(F32) + C * p
                    wc[(0, *place, slice(None), cols)] = w.astype(BF)

    def update(s):
        for n in range(K // 256):
            cols = slice(n * 256, n * 256 + 256)
            u = jnp.dot(g[s], wc[s, :, :, :, :, :, cols].reshape(S_ROWS, 256), preferred_element_type=F32)
            u += ua[:, cols] if s > 0 else A * x_ref[:, cols].astype(F32)
            if s < 7:
                ua[:, cols] = u
            else:
                o_ref[:, cols] = (FACTOR * u).astype(BF)

    hi, lo = y // 2, y % 2
    gx = [Gather(f"x{c}", xc, lambda k, c=c: (c, k)) for c in range(2)]
    gw = [
        Gather("w0", wc, lambda k: (hi, k, lo)),
        Gather("w1", wc, lambda k: (slice(None), k, 1 - lo, 0)),
        Gather("w2", wc, lambda k: (slice(None), k, 1 - lo, 1)),
        Gather("w3", wc, lambda k: (1 - hi, k, lo)),
    ]
    even, odd = (1 - lo) * Q, (3 - lo) * Q
    w0 = ([q0, q0 + H], [(hi, core, lo, 0), (hi, core, lo, 1)])
    w1 = ([even, odd], [(0, core, 1 - lo, 0), (1, core, 1 - lo, 0)])
    w2 = ([even + H, odd + H], [(0, core, 1 - lo, 1), (1, core, 1 - lo, 1)])
    w3 = ([q2, q2 + H], [(1 - hi, core, lo, 0), (1 - hi, core, lo, 1)])
    g1, g2 = GatherGram(0, CUT), GatherGram(CUT, 8)

    def each(f, units):
        for u in units:
            f(*u)

    gx[0].own()
    gx[1].own()
    each(begin, [(0, 0), (0, 1)])
    each(rs2, [(0, 0), (0, 1)])
    gx[0].near()
    gx[0].near_z()
    each(begin, [(1, 0), (2, 0), (3, 0)])
    each(rs3, [(0, 0), (0, 1)])
    each(rs2, [(1, 0), (2, 0)])
    gx[1].near()
    gx[0].pass_z()
    gx[1].near_z()
    gx[1].pass_z()
    each(begin, [(1, 1), (2, 1), (3, 1)])
    each(rs2, [(3, 0)])
    gx[0].far()
    each(begin, [(4, 0)])
    each(rs4, [(0, 0), (0, 1)])
    each(rs2, [(1, 1), (2, 1)])
    each(rs3, [(1, 0), (2, 0), (3, 0)])
    gx[1].far()
    each(begin, [(4, 1)])
    each(rs2, [(3, 1), (4, 0)])
    each(rs3, [(1, 1), (2, 1)])
    each(rs4, [(1, 0), (2, 0), (3, 0)])
    each(rs2, [(4, 1)])
    each(rs3, [(3, 1), (4, 0)])
    gx[0].far_z()
    each(begin, [(5, 0)])
    gx[0].mid()
    each(begin, [(6, 0), (7, 0)])
    each(rs3, [(4, 1)])
    each(rs2, [(5, 0)])
    each(rs4, [(1, 1), (2, 1), (3, 1), (4, 0)])
    each(rs2, [(6, 0), (7, 0)])
    each(rs3, [(5, 0)])
    gx[1].far_z()
    each(begin, [(5, 1)])
    gx[1].mid()
    each(begin, [(6, 1), (7, 1)])
    each(rs2, [(5, 1)])
    each(rs3, [(6, 0), (7, 0)])
    each(rs2, [(6, 1), (7, 1)])
    each(rs4, [(4, 1)])
    g1.own(0)
    product(*w0, 0, CUT)
    each(rs3, [(5, 1)])
    each(rs4, [(5, 0), (6, 0), (7, 0)])
    each(rs3, [(6, 1), (7, 1)])
    each(rs4, [(5, 1), (6, 1), (7, 1)])
    g2.own(0)
    g1.own(1)
    g2.own(1)
    product(*w0, CUT, 8)
    gw[0].own()
    g1.near(0)
    g2.near(0)
    gw[0].near()
    gw[0].near_z()
    gw[0].pass_z()
    product(*w1, 0, 8)
    gw[1].own()
    gw[0].far()
    gw[1].near()
    gw[1].near_z()
    gw[1].pass_z()
    gw[0].far_z()
    gw[0].mid()
    g1.near(1)
    g2.near(1)
    product(*w2, 0, 8)
    gw[2].own()
    gw[1].far()
    gw[2].near()
    gw[2].near_z()
    gw[2].pass_z()
    gw[1].far_z()
    gw[1].mid()
    g1.far()
    g2.far()
    product(*w3, 0, 8)
    gw[3].own()
    gw[2].far()
    gw[3].near()
    gw[3].near_z()
    gw[3].pass_z()
    gw[2].far_z()
    gw[2].mid()
    gw[3].far()

    def end(s):
        for part in gw:
            part.from_sib(s)
        update(s)

    for s in range(5):
        end(s)
    gw[3].far_z()
    gw[3].mid()
    for s in range(5, 8):
        end(s)

    for copy in pending[-N_SEND:]:
        copy.wait_send()
    assert len(sites) == N_RECV, len(sites)


def shards(momentum):
    unit = (8, 2, Q, HALF)
    return pl.pallas_call(
        kernel,
        out_shape=jax.ShapeDtypeStruct((R, K), BF),
        in_specs=[pl.BlockSpec(memory_space=pl.ANY)],
        out_specs=pl.BlockSpec(memory_space=pltpu.VMEM),
        scratch_shapes=[
            pltpu.VMEM((R, K), BF),
            pltpu.VMEM(SHAPE, BF),
            pltpu.VMEM(SHAPE, BF),
            pltpu.VMEM((8, 2, R, HALF), BF),
            pltpu.VMEM((8, R, S_ROWS), BF),
            pltpu.VMEM((8, 2, H, HALF), BF),
            pltpu.VMEM((8, 2, H, HALF), BF),
            pltpu.VMEM(unit, BF),
            pltpu.VMEM(unit, BF),
            pltpu.VMEM(unit, BF),
            pltpu.VMEM((R, K), F32),
            pltpu.VMEM((R, K), F32),
            pltpu.SemaphoreType.DMA((9,)),
            pltpu.SemaphoreType.DMA((N_SEND,)),
            pltpu.SemaphoreType.DMA((N_RECV,)),
        ],
        compiler_params=pltpu.CompilerParams(
            collective_id=0, has_side_effects=True, vmem_limit_bytes=58 << 20
        ),
        cost_estimate=pl.CostEstimate(flops=15 * 10**9, bytes_accessed=2 * R * K * 2, transcendentals=0),
    )(momentum)


def solution(mesh):
    placed = (P("row", "col"),)
    return jax.shard_map(
        shards, mesh=mesh, in_specs=placed, out_specs=P("row", "col"), check_vma=False
    )
```

```python
import functools
import math

import jax
import jax.numpy as jnp
from jax import lax
from jax.experimental import pallas as pl
from jax.experimental.pallas import tpu as pltpu
from jax.sharding import PartitionSpec as P

M = 6144
N = 8192
MESH = pl.DeviceIdType.MESH
BF = jnp.bfloat16
F32 = jnp.float32

A, B, C = 3.4445, -4.775, 2.0315
FACTOR = 0.2 * math.sqrt(max(M, N))

R = 384
S_ROWS = 2 * R
K = 1024
Q = R // 4
H = Q // 2

ORDER = [(0, 0), (0, 3), (0, 1), (1, 0), (0, 2), (1, 2), (1, 3), (1, 1)]
SHAPE = (8, 2, 2, 2, 2, H, K)
HALF = R
N_SEND = 56
N_RECV = 194
GROUPS = [(0, 2), (2, 5), (5, 8)]


def slot(dz, dx):
    return ORDER.index((dz % 2, dx % 4))


def kernel(x_hbm, o_ref, x_ref, xc, wc, pb, g, r1l, r1r, r2l, r2r, zr, yb, ua, local_sem, send_sem, recv_sem):
    row = lax.axis_index("row")
    col = lax.axis_index("col")
    zh, x, core = row // 8, (row % 8) // 2, row % 2
    zl, y = col // 4, col % 4

    peers = {
        "xr": {"row": zh * 8 + ((x + 1) % 4) * 2 + core},
        "xl": {"row": zh * 8 + ((x + 3) % 4) * 2 + core},
        "zp": {"row": (1 - zh) * 8 + x * 2 + core},
        "sib": {"row": zh * 8 + x * 2 + (1 - core)},
        "yr": {"col": zl * 4 + (y + 1) % 4},
        "yl": {"col": zl * 4 + (y + 3) % 4},
        "zq": {"col": (1 - zl) * 4 + y},
    }

    own_copy = pltpu.make_async_copy(x_hbm, x_ref, local_sem.at[0])
    own_copy.start()
    barrier = pltpu.get_barrier_semaphore()
    for peer in peers.values():
        pl.semaphore_signal(barrier, inc=1, device_id=peer, device_id_type=MESH)
    own_copy.wait()
    places = [
        pltpu.make_async_copy(x_ref.at[pl.ds((c * 4 + i) * H, H)], xc.at[0, c, core, i // 2, i % 2], local_sem.at[1 + c * 4 + i])
        for c in range(2) for i in range(4)
    ]
    for place in places:
        place.start()
    for place in places:
        place.wait()
    pl.semaphore_wait(barrier, len(peers))

    sites = {}
    pending = []

    def site(name):
        return sites.setdefault(name, len(sites))

    def send(name, src, dst, peer):
        i = site(name)
        n = len(pending)
        if n >= N_SEND:
            pending[n - N_SEND].wait_send()
        copy = pltpu.make_async_remote_copy(
            src_ref=src, dst_ref=dst, send_sem=send_sem.at[n % N_SEND], recv_sem=recv_sem.at[i],
            device_id=peers[peer], device_id_type=MESH,
        )
        copy.start()
        pending.append(copy)

    def recv(name, view):
        i = site(name)
        pltpu.make_async_remote_copy(
            src_ref=view, dst_ref=view, send_sem=send_sem.at[0], recv_sem=recv_sem.at[i],
            device_id=peers["sib"], device_id_type=MESH,
        ).wait_recv()

    def rows(off, n):
        return pl.ds(pl.multiple_of(off, 16), n)

    class Gather:
        def __init__(self, tag, buf, index):
            self.tag, self.buf, self.index = tag, buf, index

        def at(self, dz, dx, part=None, c=core):
            view = self.buf.at[(slot(dz, dx), *self.index(c))]
            return view if part is None else view.at[part]

        def to(self, name, dz, dx, peer, part=None):
            there = {"xr": (dz, dx - 1), "xl": (dz, dx + 1), "zp": (1 - dz, dx), "sib": (dz, dx)}[peer]
            send(self.tag + name, self.at(dz, dx, part), self.at(*there, part), peer)

        def recv(self, name, dz, dx, part=None, c=core):
            recv(self.tag + name, self.at(dz, dx, part, c))

        def own(self):
            self.to("own_r", 0, 0, "xr")
            self.to("own_l", 0, 0, "xl")
            self.to("own_z", 0, 0, "zp")
            self.to("own_s", 0, 0, "sib")

        def near(self):
            self.recv("own_r", 0, -1)
            self.to("own_rr", 0, -1, "xr", 0)
            self.to("l_s", 0, -1, "sib")
            self.recv("own_l", 0, 1)
            self.to("own_ll", 0, 1, "xl", 1)
            self.to("r_s", 0, 1, "sib")

        def near_z(self):
            self.recv("own_z", 1, 0)
            self.to("z_s", 1, 0, "sib")

        def pass_z(self):
            self.to("z_r", 1, 0, "xr")
            self.to("z_l", 1, 0, "xl")

        def far(self):
            self.recv("own_rr", 0, 2, 0)
            self.recv("own_ll", 0, 2, 1)
            self.to("f_z", 0, 2, "zp")
            self.to("f_s", 0, 2, "sib")

        def far_z(self):
            self.recv("f_z", 1, 2)
            self.to("zf_s", 1, 2, "sib")

        def mid(self):
            self.recv("z_r", 1, -1)
            self.to("zl_s", 1, -1, "sib")
            self.recv("z_l", 1, 1)
            self.to("zr_s", 1, 1, "sib")

        def from_sib(self, i):
            name = ["own_s", "l_s", "r_s", "z_s", "f_s", "zf_s", "zl_s", "zr_s"][i]
            self.recv(name, *ORDER[i], None, 1 - core)

    q0, qr, ql, q2 = y * Q, ((y + 1) % 4) * Q, ((y + 3) % 4) * Q, ((y + 2) % 4) * Q
    nt = (((1,), (1,)), ((), ()))

    def partial_gram(s, c):
        block = xc[s, c].reshape(HALF, K)
        for m in range(2):
            mine = slice(m * R // 2, (m + 1) * R // 2)
            p = lax.dot_general(x_ref[mine, :], block, nt, preferred_element_type=F32)
            pb[s, c, mine, :] = p.astype(BF)

    def add(s, c, off, n, other):
        here = (s, c, rows(off, n), slice(None))
        pb[here] = (pb[here].astype(F32) + other.astype(F32)).astype(BF)

    def begin(s, c):
        gx[c].from_sib(s)
        partial_gram(s, c)
        send(f"rs1r{s}{c}", pb.at[s, c, rows(q2, H)], r1l.at[s, c], "yr")
        send(f"rs1l{s}{c}", pb.at[s, c, rows(q2 + H, H)], r1r.at[s, c], "yl")

    def rs2(s, c):
        recv(f"rs1r{s}{c}", r1l.at[s, c])
        add(s, c, qr, H, r1l[s, c])
        send(f"rs2r{s}{c}", pb.at[s, c, rows(qr, Q)], r2l.at[s, c], "yr")
        recv(f"rs1l{s}{c}", r1r.at[s, c])
        add(s, c, ql + H, H, r1r[s, c])
        send(f"rs2l{s}{c}", pb.at[s, c, rows(ql, Q)], r2r.at[s, c], "yl")

    def rs3(s, c):
        recv(f"rs2r{s}{c}", r2l.at[s, c])
        recv(f"rs2l{s}{c}", r2r.at[s, c])
        add(s, c, q0, Q, r2l[s, c].astype(F32) + r2r[s, c].astype(F32))
        send(f"rs3{s}{c}", pb.at[s, c, rows(q0, Q)], zr.at[s, c], "zq")

    def rs4(s, c):
        recv(f"rs3{s}{c}", zr.at[s, c])
        total = pb[s, c, rows(q0, Q), :].astype(F32) + zr[s, c].astype(F32)
        g[s, rows(q0, Q), c * HALF : (c + 1) * HALF] = total.astype(BF)

    class GatherGram:
        def __init__(self, s0, s1):
            self.s0, self.s1 = s0, s1

        def at(self, off, t):
            return g.at[self.s0 : self.s1, rows(off + t * H, H)]

        def own(self, t):
            send(f"g_r{self.s0}{t}", self.at(q0, t), self.at(q0, t), "yr")
            send(f"g_l{self.s0}{t}", self.at(q0, t), self.at(q0, t), "yl")

        def near(self, t):
            recv(f"g_r{self.s0}{t}", self.at(ql, t))
            recv(f"g_l{self.s0}{t}", self.at(qr, t))
            if t == 0:
                send(f"g_rr{self.s0}", self.at(ql, 0), self.at(ql, 0), "yr")
            else:
                send(f"g_ll{self.s0}", self.at(qr, 1), self.at(qr, 1), "yl")

        def far(self):
            recv(f"g_rr{self.s0}", self.at(q2, 0))
            recv(f"g_ll{self.s0}", self.at(q2, 1))

    def product(offs, places, s0, s1):
        for n in range(K // 256):
            cols = slice(n * 256, n * 256 + 256)
            part = None
            for s in range(s0, s1):
                lhs = jnp.concatenate([g[s, rows(off, H), :] for off in offs], axis=0)
                rhs = xc[s, :, :, :, :, :, cols].reshape(S_ROWS, 256)
                d = jnp.dot(lhs, rhs, preferred_element_type=F32)
                part = d if part is None else part + d
            for j, (off, place) in enumerate(zip(offs, places)):
                p = part[j * H : (j + 1) * H]
                if s0 > 0:
                    p += yb[rows(off, H), cols]
                if s1 < 8:
                    yb[rows(off, H), cols] = p
                else:
                    w = B * x_ref[rows(off, H), cols].astype(F32) + C * p
                    wc[(0, *place, slice(None), cols)] = w.astype(BF)

    def update(s):
        for n in range(K // 256):
            cols = slice(n * 256, n * 256 + 256)
            u = jnp.dot(g[s], wc[s, :, :, :, :, :, cols].reshape(S_ROWS, 256), preferred_element_type=F32)
            u += ua[:, cols] if s != 1 else A * x_ref[:, cols].astype(F32)
            if s != 5:
                ua[:, cols] = u
            else:
                o_ref[:, cols] = (FACTOR * u).astype(BF)

    hi, lo = y // 2, y % 2
    gx = [Gather(f"x{c}", xc, lambda k, c=c: (c, k)) for c in range(2)]
    gw = [
        Gather("w0", wc, lambda k: (hi, k, lo)),
        Gather("w1", wc, lambda k: (slice(None), k, 1 - lo, 0)),
        Gather("w2", wc, lambda k: (slice(None), k, 1 - lo, 1)),
        Gather("w3", wc, lambda k: (1 - hi, k, lo)),
    ]
    even, odd = (1 - lo) * Q, (3 - lo) * Q
    w0 = ([q0, q0 + H], [(hi, core, lo, 0), (hi, core, lo, 1)])
    w1 = ([even, odd], [(0, core, 1 - lo, 0), (1, core, 1 - lo, 0)])
    w2 = ([even + H, odd + H], [(0, core, 1 - lo, 1), (1, core, 1 - lo, 1)])
    w3 = ([q2, q2 + H], [(1 - hi, core, lo, 0), (1 - hi, core, lo, 1)])
    gg = [GatherGram(s0, s1) for s0, s1 in GROUPS]

    def each(f, units):
        for u in units:
            f(*u)

    def end(s):
        for part in gw:
            part.from_sib(s)
        update(s)

    gx[0].own()
    gx[1].own()
    each(begin, [(0, 1), (0, 0)])
    each(rs2, [(0, 0)])
    gx[0].near()
    gx[0].near_z()
    each(begin, [(2, 0), (1, 0)])
    each(rs2, [(0, 1)])
    each(rs3, [(0, 0)])
    each(rs2, [(1, 0)])
    each(begin, [(3, 0)])
    each(rs3, [(0, 1)])
    each(rs2, [(2, 0)])
    gx[1].near()
    each(begin, [(1, 1)])
    each(rs3, [(1, 0)])
    gx[1].near_z()
    each(rs2, [(3, 0)])
    each(begin, [(2, 1)])
    gx[0].far()
    each(begin, [(3, 1)])
    each(rs4, [(0, 0)])
    gx[0].pass_z()
    each(rs2, [(1, 1)])
    each(begin, [(4, 0)])
    each(rs2, [(3, 1)])
    gx[1].far()
    each(begin, [(4, 1)])
    each(rs3, [(1, 1)])
    each(rs4, [(0, 1)])
    each(rs2, [(4, 0), (2, 1)])
    each(rs3, [(3, 0)])
    each(rs2, [(4, 1)])
    gx[1].pass_z()
    gx[0].far_z()
    gx[0].mid()
    each(begin, [(7, 0), (6, 0)])
    each(rs3, [(2, 1)])
    each(begin, [(5, 0)])
    each(rs2, [(7, 0), (5, 0)])
    each(rs3, [(2, 0)])
    each(rs2, [(6, 0)])
    gx[1].far_z()
    gx[1].mid()
    each(rs4, [(1, 0), (1, 1)])
    each(rs3, [(4, 0)])
    each(begin, [(5, 1)])
    each(rs3, [(3, 1)])
    each(begin, [(6, 1)])
    gg[0].own(0)
    each(begin, [(7, 1)])
    each(rs4, [(2, 0), (2, 1)])
    each(rs3, [(4, 1), (5, 0)])
    each(rs2, [(5, 1), (6, 1)])
    product(*w0, 0, 2)
    each(rs2, [(7, 1)])
    each(rs3, [(7, 0)])
    each(rs4, [(4, 0), (3, 1)])
    each(rs3, [(5, 1)])
    each(rs4, [(3, 0)])
    gg[0].own(1)
    each(rs3, [(6, 1)])
    each(rs4, [(4, 1)])
    gg[1].own(1)
    gg[1].own(0)
    each(rs4, [(5, 0)])
    each(rs3, [(7, 1)])
    product(*w0, 2, 5)
    each(rs4, [(6, 1), (7, 0)])
    each(rs3, [(6, 0)])
    each(rs4, [(7, 1), (5, 1), (6, 0)])
    gg[2].own(0)
    gg[2].own(1)
    product(*w0, 5, 8)
    gw[0].own()
    gg[0].near(0)
    gg[0].near(1)
    gg[1].near(1)
    product(*w2, 0, 5)
    gw[0].near()
    product(*w1, 0, 2)
    gw[0].near_z()
    gg[1].near(0)
    product(*w1, 2, 5)
    gw[0].pass_z()
    gg[2].near(0)
    product(*w1, 5, 8)
    gw[1].own()
    gw[0].mid()
    gg[2].near(1)
    product(*w2, 5, 8)
    gw[2].own()
    gw[0].far()
    gw[1].near()
    gg[0].far()
    product(*w3, 0, 2)
    gw[1].near_z()
    gw[1].pass_z()
    gg[1].far()
    product(*w3, 2, 5)
    gw[2].near_z()
    gw[2].near()
    gw[1].far()
    gg[2].far()
    product(*w3, 5, 8)
    gw[3].own()
    gw[2].far()
    gw[1].far_z()
    gw[2].pass_z()
    gw[0].far_z()
    gw[3].near()
    gw[3].near_z()
    gw[3].pass_z()
    end(1)
    end(0)
    end(2)
    gw[3].far()
    gw[2].far_z()
    gw[1].mid()
    end(3)
    end(4)
    gw[2].mid()
    gw[3].mid()
    end(6)
    gw[3].far_z()
    end(7)
    end(5)

    for copy in pending[-N_SEND:]:
        copy.wait_send()
    assert len(sites) == N_RECV, len(sites)


def shards(momentum):
    unit = (8, 2, Q, HALF)
    return pl.pallas_call(
        kernel,
        out_shape=jax.ShapeDtypeStruct((R, K), BF),
        in_specs=[pl.BlockSpec(memory_space=pl.ANY)],
        out_specs=pl.BlockSpec(memory_space=pltpu.VMEM),
        scratch_shapes=[
            pltpu.VMEM((R, K), BF),
            pltpu.VMEM(SHAPE, BF),
            pltpu.VMEM(SHAPE, BF),
            pltpu.VMEM((8, 2, R, HALF), BF),
            pltpu.VMEM((8, R, S_ROWS), BF),
            pltpu.VMEM((8, 2, H, HALF), BF),
            pltpu.VMEM((8, 2, H, HALF), BF),
            pltpu.VMEM(unit, BF),
            pltpu.VMEM(unit, BF),
            pltpu.VMEM(unit, BF),
            pltpu.VMEM((R, K), F32),
            pltpu.VMEM((R, K), F32),
            pltpu.SemaphoreType.DMA((9,)),
            pltpu.SemaphoreType.DMA((N_SEND,)),
            pltpu.SemaphoreType.DMA((N_RECV,)),
        ],
        compiler_params=pltpu.CompilerParams(
            collective_id=0, has_side_effects=True, vmem_limit_bytes=58 << 20
        ),
        cost_estimate=pl.CostEstimate(flops=15 * 10**9, bytes_accessed=2 * R * K * 2, transcendentals=0),
    )(momentum)


def solution(mesh):
    placed = (P("row", "col"),)
    return jax.shard_map(
        shards, mesh=mesh, in_specs=placed, out_specs=P("row", "col"), check_vma=False
    )
```

```python
import functools
import math

import jax
import jax.numpy as jnp
from jax import lax
from jax.experimental import pallas as pl
from jax.experimental.pallas import tpu as pltpu
from jax.sharding import PartitionSpec as P

M = 6144
N = 8192
MESH = pl.DeviceIdType.MESH
BF = jnp.bfloat16
F32 = jnp.float32

A, B, C = 3.4445, -4.775, 2.0315
FACTOR = 0.2 * math.sqrt(max(M, N))

R = 384
S_ROWS = 2 * R
K = 1024
Q = R // 4
H = Q // 2

ORDER = [(0, 0), (0, 3), (0, 1), (1, 0), (0, 2), (1, 2), (1, 3), (1, 1)]
SHAPE = (8, 2, 2, 2, 2, H, K)
HALF = R
N_SEND = 56
N_RECV = 182
MODES = {"x0": "B", "x1": "B", "w0": "B", "w1": "C", "w2": "B", "w3": "A"}
GROUPS = [(0, 2), (2, 5), (5, 8)]


def slot(dz, dx):
    return ORDER.index((dz % 2, dx % 4))


def kernel(x_hbm, o_ref, x_ref, xc, wc, pb, g, r1l, r1r, r2l, r2r, zr, yb, ua, local_sem, send_sem, recv_sem):
    row = lax.axis_index("row")
    col = lax.axis_index("col")
    zh, x, core = row // 8, (row % 8) // 2, row % 2
    zl, y = col // 4, col % 4

    peers = {
        "xr": {"row": zh * 8 + ((x + 1) % 4) * 2 + core},
        "xl": {"row": zh * 8 + ((x + 3) % 4) * 2 + core},
        "zp": {"row": (1 - zh) * 8 + x * 2 + core},
        "sib": {"row": zh * 8 + x * 2 + (1 - core)},
        "yr": {"col": zl * 4 + (y + 1) % 4},
        "yl": {"col": zl * 4 + (y + 3) % 4},
        "zq": {"col": (1 - zl) * 4 + y},
    }

    copies = [pltpu.make_async_copy(x_hbm, x_ref, local_sem.at[0])]
    for i in range(8):
        place = xc.at[0, i // 4, core, i // 2 % 2, i % 2]
        copies.append(pltpu.make_async_copy(x_hbm.at[pl.ds(i * H, H)], place, local_sem.at[1 + i]))
    for copy in copies:
        copy.start()
    barrier = pltpu.get_barrier_semaphore()
    for peer in peers.values():
        pl.semaphore_signal(barrier, inc=1, device_id=peer, device_id_type=MESH)
    for copy in copies:
        copy.wait()
    pl.semaphore_wait(barrier, len(peers))

    sites = {}
    pending = []

    def site(name):
        return sites.setdefault(name, len(sites))

    def send(name, src, dst, peer):
        i = site(name)
        n = len(pending)
        if n >= N_SEND:
            pending[n - N_SEND].wait_send()
        copy = pltpu.make_async_remote_copy(
            src_ref=src, dst_ref=dst, send_sem=send_sem.at[n % N_SEND], recv_sem=recv_sem.at[i],
            device_id=peers[peer], device_id_type=MESH,
        )
        copy.start()
        pending.append(copy)

    def recv(name, view):
        i = site(name)
        pltpu.make_async_remote_copy(
            src_ref=view, dst_ref=view, send_sem=send_sem.at[0], recv_sem=recv_sem.at[i],
            device_id=peers["sib"], device_id_type=MESH,
        ).wait_recv()

    def rows(off, n):
        return pl.ds(pl.multiple_of(off, 16), n)

    class Gather:
        def __init__(self, tag, buf, index):
            self.tag, self.buf, self.index, self.seen = tag, buf, index, set()
            self.mode = MODES[tag]

        def at(self, dz, dx, part=None, c=core):
            view = self.buf.at[(slot(dz, dx), *self.index(c))]
            return view if part is None else view.at[part]

        def to(self, name, dz, dx, peer, part=None):
            there = {"xr": (dz, dx - 1), "xl": (dz, dx + 1), "zp": (1 - dz, dx), "sib": (dz, dx)}[peer]
            send(self.tag + name, self.at(dz, dx, part), self.at(*there, part), peer)

        def recv(self, name, dz, dx, part=None, c=core):
            recv(self.tag + name, self.at(dz, dx, part, c))

        def own(self):
            self.to("own_r", 0, 0, "xr")
            self.to("own_l", 0, 0, "xl")
            self.to("own_z", 0, 0, "zp")
            self.to("own_s", 0, 0, "sib")

        def near(self):
            self.recv("own_r", 0, -1)
            self.to("own_rr", 0, -1, "xr", 0)
            self.recv("own_l", 0, 1)
            self.to("own_ll", 0, 1, "xl", 1)
            self.both("lr_s", 1)
            if self.mode == "C":
                send(self.tag + "lr_z", self.pair(1, core), self.pair(6, core), "zp")
            if self.mode == "H":
                send(self.tag + "lr_z", self.pair(1, core, 1), self.pair(6, core, 1), "zp")

        def near_z(self):
            self.recv("own_z", 1, 0)
            self.to("z_s", 1, 0, "sib")

        def pass_z(self):
            if self.mode != "C":
                part = 0 if self.mode == "H" else None
                self.to("z_r", 1, 0, "xr", part)
                self.to("z_l", 1, 0, "xl", part)

        def far(self):
            self.recv("own_rr", 0, 2, 0)
            self.recv("own_ll", 0, 2, 1)
            if self.mode != "A":
                self.to("f_z", 0, 2, "zp")
            self.to("f_s", 0, 2, "sib")

        def far_z(self):
            if self.mode == "A":
                self.recv("z_rr", 1, 2, 0)
                self.recv("z_ll", 1, 2, 1)
            else:
                self.recv("f_z", 1, 2)
            self.to("zf_s", 1, 2, "sib")

        def mid(self):
            part = 0 if self.mode == "H" else None
            if self.mode != "C":
                self.recv("z_r", 1, -1, part)
                if self.mode == "A":
                    self.to("z_rr", 1, -1, "xr", 0)
                self.recv("z_l", 1, 1, part)
                if self.mode == "A":
                    self.to("z_ll", 1, 1, "xl", 1)
            if self.mode == "C":
                recv(self.tag + "lr_z", self.pair(6, core))
            if self.mode == "H":
                recv(self.tag + "lr_z", self.pair(6, core, 1))
            self.both("zlr_s", 6)

        def pair(self, i, c, part=None):
            view = self.buf.at[(slice(i, i + 2), *self.index(c))]
            return view if part is None else view.at[:, part]

        def both(self, name, i):
            send(self.tag + name, self.pair(i, core), self.pair(i, core), "sib")

        def from_sib(self, i):
            name = ["own_s", "lr_s", "lr_s", "z_s", "f_s", "zf_s", "zlr_s", "zlr_s"][i]
            if name in self.seen:
                return
            self.seen.add(name)
            if name in ("lr_s", "zlr_s"):
                recv(self.tag + name, self.pair(i // 5 * 5 + 1, 1 - core))
            else:
                self.recv(name, *ORDER[i], None, 1 - core)

    q0, qr, ql, q2 = y * Q, ((y + 1) % 4) * Q, ((y + 3) % 4) * Q, ((y + 2) % 4) * Q
    nt = (((1,), (1,)), ((), ()))

    def partial_gram(s, c):
        block = xc[s, c].reshape(HALF, K)
        for m in range(2):
            mine = slice(m * R // 2, (m + 1) * R // 2)
            p = lax.dot_general(x_ref[mine, :], block, nt, preferred_element_type=F32)
            pb[s, c, mine, :] = p.astype(BF)

    def add(s, c, off, n, other):
        here = (s, c, rows(off, n), slice(None))
        pb[here] = (pb[here].astype(F32) + other.astype(F32)).astype(BF)

    def begin(s, c):
        gx[c].from_sib(s)
        partial_gram(s, c)
        send(f"rs1r{s}{c}", pb.at[s, c, rows(q2, H)], r1l.at[s, c], "yr")
        send(f"rs1l{s}{c}", pb.at[s, c, rows(q2 + H, H)], r1r.at[s, c], "yl")

    def rs2(s, c):
        recv(f"rs1r{s}{c}", r1l.at[s, c])
        add(s, c, qr, H, r1l[s, c])
        send(f"rs2r{s}{c}", pb.at[s, c, rows(qr, Q)], r2l.at[s, c], "yr")
        recv(f"rs1l{s}{c}", r1r.at[s, c])
        add(s, c, ql + H, H, r1r[s, c])
        send(f"rs2l{s}{c}", pb.at[s, c, rows(ql, Q)], r2r.at[s, c], "yl")

    def rs3(s, c):
        recv(f"rs2r{s}{c}", r2l.at[s, c])
        recv(f"rs2l{s}{c}", r2r.at[s, c])
        add(s, c, q0, Q, r2l[s, c].astype(F32) + r2r[s, c].astype(F32))
        send(f"rs3{s}{c}", pb.at[s, c, rows(q0, Q)], zr.at[s, c], "zq")

    def rs4(s, c):
        recv(f"rs3{s}{c}", zr.at[s, c])
        total = pb[s, c, rows(q0, Q), :].astype(F32) + zr[s, c].astype(F32)
        g[s, rows(q0, Q), c * HALF : (c + 1) * HALF] = total.astype(BF)

    class GatherGram:
        def __init__(self, s0, s1):
            self.s0, self.s1 = s0, s1

        def at(self, off, t):
            return g.at[self.s0 : self.s1, rows(off + t * H, H)]

        def own(self, t):
            send(f"g_r{self.s0}{t}", self.at(q0, t), self.at(q0, t), "yr")
            send(f"g_l{self.s0}{t}", self.at(q0, t), self.at(q0, t), "yl")

        def near(self, t):
            recv(f"g_r{self.s0}{t}", self.at(ql, t))
            recv(f"g_l{self.s0}{t}", self.at(qr, t))
            if t == 0:
                send(f"g_rr{self.s0}", self.at(ql, 0), self.at(ql, 0), "yr")
            else:
                send(f"g_ll{self.s0}", self.at(qr, 1), self.at(qr, 1), "yl")

        def far(self):
            recv(f"g_rr{self.s0}", self.at(q2, 0))
            recv(f"g_ll{self.s0}", self.at(q2, 1))

    def product(offs, places, s0, s1):
        for n in range(K // 256):
            cols = slice(n * 256, n * 256 + 256)
            part = None
            for s in range(s0, s1):
                lhs = jnp.concatenate([g[s, rows(off, H), :] for off in offs], axis=0)
                rhs = xc[s, :, :, :, :, :, cols].reshape(S_ROWS, 256)
                d = jnp.dot(lhs, rhs, preferred_element_type=F32)
                part = d if part is None else part + d
            for j, (off, place) in enumerate(zip(offs, places)):
                p = part[j * H : (j + 1) * H]
                if s0 > 0:
                    p += yb[rows(off, H), cols]
                if s1 < 8:
                    yb[rows(off, H), cols] = p
                else:
                    w = B * x_ref[rows(off, H), cols].astype(F32) + C * p
                    wc[(0, *place, slice(None), cols)] = w.astype(BF)

    def update(s):
        for n in range(K // 256):
            cols = slice(n * 256, n * 256 + 256)
            u = jnp.dot(g[s], wc[s, :, :, :, :, :, cols].reshape(S_ROWS, 256), preferred_element_type=F32)
            u += ua[:, cols] if s != 0 else A * x_ref[:, cols].astype(F32)
            if s != 5:
                ua[:, cols] = u
            else:
                o_ref[:, cols] = (FACTOR * u).astype(BF)

    hi, lo = y // 2, y % 2
    gx = [Gather(f"x{c}", xc, lambda k, c=c: (c, k)) for c in range(2)]
    gw = [
        Gather("w0", wc, lambda k: (hi, k, lo)),
        Gather("w1", wc, lambda k: (slice(None), k, 1 - lo, 0)),
        Gather("w2", wc, lambda k: (slice(None), k, 1 - lo, 1)),
        Gather("w3", wc, lambda k: (1 - hi, k, lo)),
    ]
    even, odd = (1 - lo) * Q, (3 - lo) * Q
    w0 = ([q0, q0 + H], [(hi, core, lo, 0), (hi, core, lo, 1)])
    w1 = ([even, odd], [(0, core, 1 - lo, 0), (1, core, 1 - lo, 0)])
    w2 = ([even + H, odd + H], [(0, core, 1 - lo, 1), (1, core, 1 - lo, 1)])
    w3 = ([q2, q2 + H], [(1 - hi, core, lo, 0), (1 - hi, core, lo, 1)])
    gg = [GatherGram(s0, s1) for s0, s1 in GROUPS]

    def each(f, units):
        for u in units:
            f(*u)

    def end(s):
        for part in gw:
            part.from_sib(s)
        update(s)

    gx[0].own()
    gx[1].own()
    each(begin, [(0, 0), (0, 1)])
    gx[0].near()
    each(rs2, [(0, 1)])
    each(begin, [(1, 0)])
    each(rs2, [(0, 0)])
    each(begin, [(2, 0)])
    each(rs3, [(0, 1)])
    each(rs2, [(1, 0)])
    gx[0].near_z()
    each(begin, [(3, 0)])
    gx[1].near_z()
    each(rs3, [(0, 0)])
    gx[1].near()
    gx[0].pass_z()
    each(rs2, [(2, 0)])
    each(rs3, [(1, 0)])
    each(rs2, [(3, 0)])
    gx[0].far()
    each(begin, [(1, 1), (3, 1), (2, 1)])
    gx[1].pass_z()
    each(begin, [(4, 0)])
    each(rs2, [(1, 1)])
    each(rs4, [(0, 1)])
    gx[1].far()
    each(begin, [(4, 1)])
    each(rs2, [(2, 1), (3, 1), (4, 0), (4, 1)])
    gx[0].far_z()
    gx[0].mid()
    each(begin, [(5, 0), (6, 0)])
    each(rs3, [(1, 1), (4, 1), (3, 1)])
    each(begin, [(7, 0)])
    each(rs2, [(5, 0), (6, 0), (7, 0)])
    gx[1].far_z()
    each(rs3, [(2, 1), (2, 0)])
    each(begin, [(5, 1)])
    each(rs4, [(1, 0), (4, 1)])
    each(rs3, [(3, 0)])
    each(rs4, [(1, 1), (0, 0)])
    gx[1].mid()
    each(rs3, [(4, 0)])
    gg[0].own(0)
    each(rs3, [(5, 0)])
    each(begin, [(7, 1)])
    each(rs4, [(2, 1)])
    each(rs3, [(7, 0)])
    product(*w0, 0, 2)
    each(rs4, [(3, 1)])
    each(begin, [(6, 1)])
    each(rs2, [(5, 1)])
    each(rs3, [(6, 0)])
    each(rs4, [(3, 0)])
    each(rs2, [(7, 1)])
    each(rs4, [(2, 0)])
    each(rs2, [(6, 1)])
    each(rs4, [(4, 0)])
    each(rs3, [(5, 1)])
    gg[1].own(0)
    each(rs3, [(7, 1)])
    each(rs4, [(7, 0)])
    gg[0].own(1)
    each(rs3, [(6, 1)])
    product(*w0, 2, 5)
    each(rs4, [(6, 0), (7, 1), (5, 0), (5, 1), (6, 1)])
    product(*w0, 5, 8)
    gg[2].own(0)
    gw[0].own()
    gg[1].own(1)
    gg[2].own(1)
    gg[0].near(0)
    gg[0].near(1)
    product(*w1, 0, 2)
    gw[0].near()
    gg[1].near(0)
    gg[2].near(0)
    product(*w1, 2, 8)
    gw[1].own()
    product(*w2, 0, 2)
    gg[1].near(1)
    gw[0].near_z()
    gw[0].pass_z()
    product(*w2, 2, 5)
    gw[0].far()
    gw[1].near_z()
    gg[2].near(1)
    product(*w2, 5, 8)
    gw[2].own()
    gw[1].pass_z()
    gg[0].far()
    gw[1].near()
    gw[2].near()
    gw[2].near_z()
    gw[2].pass_z()
    product(*w3, 0, 2)
    gg[1].far()
    product(*w3, 2, 5)
    gg[2].far()
    product(*w3, 5, 8)
    gw[3].own()
    gw[0].mid()
    end(0)
    gw[1].far()
    gw[3].near_z()
    gw[3].pass_z()
    gw[3].near()
    gw[0].far_z()
    end(3)
    gw[2].mid()
    end(1)
    gw[2].far()
    gw[1].mid()
    gw[1].far_z()
    end(2)
    gw[3].mid()
    end(7)
    gw[3].far()
    end(6)
    gw[2].far_z()
    gw[3].far_z()
    end(4)
    end(5)

    for copy in pending[-N_SEND:]:
        copy.wait_send()
    assert len(sites) == N_RECV, len(sites)


def shards(momentum):
    unit = (8, 2, Q, HALF)
    return pl.pallas_call(
        kernel,
        out_shape=jax.ShapeDtypeStruct((R, K), BF),
        in_specs=[pl.BlockSpec(memory_space=pl.ANY)],
        out_specs=pl.BlockSpec(memory_space=pltpu.VMEM),
        scratch_shapes=[
            pltpu.VMEM((R, K), BF),
            pltpu.VMEM(SHAPE, BF),
            pltpu.VMEM(SHAPE, BF),
            pltpu.VMEM((8, 2, R, HALF), BF),
            pltpu.VMEM((8, R, S_ROWS), BF),
            pltpu.VMEM((8, 2, H, HALF), BF),
            pltpu.VMEM((8, 2, H, HALF), BF),
            pltpu.VMEM(unit, BF),
            pltpu.VMEM(unit, BF),
            pltpu.VMEM(unit, BF),
            pltpu.VMEM((R, K), F32),
            pltpu.VMEM((R, K), F32),
            pltpu.SemaphoreType.DMA((9,)),
            pltpu.SemaphoreType.DMA((N_SEND,)),
            pltpu.SemaphoreType.DMA((N_RECV,)),
        ],
        compiler_params=pltpu.CompilerParams(
            collective_id=0, has_side_effects=True, vmem_limit_bytes=58 << 20
        ),
        cost_estimate=pl.CostEstimate(flops=15 * 10**9, bytes_accessed=2 * R * K * 2, transcendentals=0),
    )(momentum)


def solution(mesh):
    placed = (P("row", "col"),)
    return jax.shard_map(
        shards, mesh=mesh, in_specs=placed, out_specs=P("row", "col"), check_vma=False
    )
```

```python
import functools
import math

import jax
import jax.numpy as jnp
from jax import lax
from jax.experimental import pallas as pl
from jax.experimental.pallas import tpu as pltpu
from jax.sharding import PartitionSpec as P

M = 6144
N = 8192
MESH = pl.DeviceIdType.MESH
BF = jnp.bfloat16
F32 = jnp.float32

A, B, C = 3.4445, -4.775, 2.0315
FACTOR = 0.2 * math.sqrt(max(M, N))

R = 384
S_ROWS = 2 * R
K = 1024
Q = R // 4
H = Q // 2

ORDER = [(0, 0), (0, 3), (0, 1), (1, 0), (0, 2), (1, 2), (1, 3), (1, 1)]
SHAPE = (8, 2, 2, 2, 2, H, K)
HALF = R
N_SEND = 40
N_RECV = 182
MODES = {"x0": "B", "x1": "B", "w0": "B", "w1": "C", "w2": "B", "w3": "A"}
GROUPS = [(0, 2), (2, 5), (5, 8)]


def slot(dz, dx):
    return ORDER.index((dz % 2, dx % 4))


def kernel(x_hbm, o_ref, x_ref, xc, wc, pb, g, r1l, r1r, r2l, r2r, zr, yb, ua, local_sem, send_sem, recv_sem):
    row = lax.axis_index("row")
    col = lax.axis_index("col")
    zh, x, core = row // 8, (row % 8) // 2, row % 2
    zl, y = col // 4, col % 4

    peers = {
        "xr": {"row": zh * 8 + ((x + 1) % 4) * 2 + core},
        "xl": {"row": zh * 8 + ((x + 3) % 4) * 2 + core},
        "zp": {"row": (1 - zh) * 8 + x * 2 + core},
        "sib": {"row": zh * 8 + x * 2 + (1 - core)},
        "yr": {"col": zl * 4 + (y + 1) % 4},
        "yl": {"col": zl * 4 + (y + 3) % 4},
        "zq": {"col": (1 - zl) * 4 + y},
    }

    copies = [pltpu.make_async_copy(x_hbm, x_ref, local_sem.at[0])]
    for i in range(8):
        place = xc.at[0, i // 4, core, i // 2 % 2, i % 2]
        copies.append(pltpu.make_async_copy(x_hbm.at[pl.ds(i * H, H)], place, local_sem.at[1 + i]))
    for copy in copies:
        copy.start()
    barrier = pltpu.get_barrier_semaphore()
    for peer in peers.values():
        pl.semaphore_signal(barrier, inc=1, device_id=peer, device_id_type=MESH)
    for copy in copies:
        copy.wait()
    pl.semaphore_wait(barrier, len(peers))

    sites = {}
    pending = []

    def site(name):
        return sites.setdefault(name, len(sites))

    def send(name, src, dst, peer):
        i = site(name)
        n = len(pending)
        if n >= N_SEND:
            pending[n - N_SEND].wait_send()
        copy = pltpu.make_async_remote_copy(
            src_ref=src, dst_ref=dst, send_sem=send_sem.at[n % N_SEND], recv_sem=recv_sem.at[i],
            device_id=peers[peer], device_id_type=MESH,
        )
        copy.start()
        pending.append(copy)

    def recv(name, view):
        i = site(name)
        pltpu.make_async_remote_copy(
            src_ref=view, dst_ref=view, send_sem=send_sem.at[0], recv_sem=recv_sem.at[i],
            device_id=peers["sib"], device_id_type=MESH,
        ).wait_recv()

    def rows(off, n):
        return pl.ds(pl.multiple_of(off, 16), n)

    class Gather:
        def __init__(self, tag, buf, index):
            self.tag, self.buf, self.index, self.seen = tag, buf, index, set()
            self.mode = MODES[tag]

        def at(self, dz, dx, part=None, c=core):
            view = self.buf.at[(slot(dz, dx), *self.index(c))]
            return view if part is None else view.at[part]

        def to(self, name, dz, dx, peer, part=None):
            there = {"xr": (dz, dx - 1), "xl": (dz, dx + 1), "zp": (1 - dz, dx), "sib": (dz, dx)}[peer]
            send(self.tag + name, self.at(dz, dx, part), self.at(*there, part), peer)

        def recv(self, name, dz, dx, part=None, c=core):
            recv(self.tag + name, self.at(dz, dx, part, c))

        def own(self):
            self.to("own_r", 0, 0, "xr")
            self.to("own_l", 0, 0, "xl")
            self.to("own_z", 0, 0, "zp")
            self.to("own_s", 0, 0, "sib")

        def near(self):
            self.recv("own_r", 0, -1)
            self.to("own_rr", 0, -1, "xr", 0)
            self.recv("own_l", 0, 1)
            self.to("own_ll", 0, 1, "xl", 1)
            self.both("lr_s", 1)
            if self.mode == "C":
                send(self.tag + "lr_z", self.pair(1, core), self.pair(6, core), "zp")
            if self.mode == "H":
                send(self.tag + "lr_z", self.pair(1, core, 1), self.pair(6, core, 1), "zp")

        def near_z(self):
            self.recv("own_z", 1, 0)
            self.to("z_s", 1, 0, "sib")

        def pass_z(self):
            if self.mode != "C":
                part = 0 if self.mode == "H" else None
                self.to("z_r", 1, 0, "xr", part)
                self.to("z_l", 1, 0, "xl", part)

        def far(self):
            self.recv("own_rr", 0, 2, 0)
            self.recv("own_ll", 0, 2, 1)
            if self.mode != "A":
                self.to("f_z", 0, 2, "zp")
            self.to("f_s", 0, 2, "sib")

        def far_z(self):
            if self.mode == "A":
                self.recv("z_rr", 1, 2, 0)
                self.recv("z_ll", 1, 2, 1)
            else:
                self.recv("f_z", 1, 2)
            self.to("zf_s", 1, 2, "sib")

        def mid(self):
            part = 0 if self.mode == "H" else None
            if self.mode != "C":
                self.recv("z_r", 1, -1, part)
                if self.mode == "A":
                    self.to("z_rr", 1, -1, "xr", 0)
                self.recv("z_l", 1, 1, part)
                if self.mode == "A":
                    self.to("z_ll", 1, 1, "xl", 1)
            if self.mode == "C":
                recv(self.tag + "lr_z", self.pair(6, core))
            if self.mode == "H":
                recv(self.tag + "lr_z", self.pair(6, core, 1))
            self.both("zlr_s", 6)

        def pair(self, i, c, part=None):
            view = self.buf.at[(slice(i, i + 2), *self.index(c))]
            return view if part is None else view.at[:, part]

        def both(self, name, i):
            send(self.tag + name, self.pair(i, core), self.pair(i, core), "sib")

        def from_sib(self, i):
            name = ["own_s", "lr_s", "lr_s", "z_s", "f_s", "zf_s", "zlr_s", "zlr_s"][i]
            if name in self.seen:
                return
            self.seen.add(name)
            if name in ("lr_s", "zlr_s"):
                recv(self.tag + name, self.pair(i // 5 * 5 + 1, 1 - core))
            else:
                self.recv(name, *ORDER[i], None, 1 - core)

    q0, qr, ql, q2 = y * Q, ((y + 1) % 4) * Q, ((y + 3) % 4) * Q, ((y + 2) % 4) * Q
    nt = (((1,), (1,)), ((), ()))

    def partial_gram(s, c):
        block = xc[s, c].reshape(HALF, K)
        for m in range(2):
            mine = slice(m * R // 2, (m + 1) * R // 2)
            p = lax.dot_general(x_ref[mine, :], block, nt, preferred_element_type=F32)
            pb[s, c, mine, :] = p.astype(BF)

    def add(s, c, off, n, other):
        here = (s, c, rows(off, n), slice(None))
        pb[here] = (pb[here].astype(F32) + other.astype(F32)).astype(BF)

    def begin(s, c):
        gx[c].from_sib(s)
        partial_gram(s, c)
        send(f"rs1r{s}{c}", pb.at[s, c, rows(q2, H)], r1l.at[s, c], "yr")
        send(f"rs1l{s}{c}", pb.at[s, c, rows(q2 + H, H)], r1r.at[s, c], "yl")

    def rs2(s, c):
        recv(f"rs1r{s}{c}", r1l.at[s, c])
        add(s, c, qr, H, r1l[s, c])
        send(f"rs2r{s}{c}", pb.at[s, c, rows(qr, Q)], r2l.at[s, c], "yr")
        recv(f"rs1l{s}{c}", r1r.at[s, c])
        add(s, c, ql + H, H, r1r[s, c])
        send(f"rs2l{s}{c}", pb.at[s, c, rows(ql, Q)], r2r.at[s, c], "yl")

    def rs3(s, c):
        recv(f"rs2r{s}{c}", r2l.at[s, c])
        recv(f"rs2l{s}{c}", r2r.at[s, c])
        add(s, c, q0, Q, r2l[s, c].astype(F32) + r2r[s, c].astype(F32))
        send(f"rs3{s}{c}", pb.at[s, c, rows(q0, Q)], zr.at[s, c], "zq")

    def rs4(s, c):
        recv(f"rs3{s}{c}", zr.at[s, c])
        total = pb[s, c, rows(q0, Q), :].astype(F32) + zr[s, c].astype(F32)
        g[s, rows(q0, Q), c * HALF : (c + 1) * HALF] = total.astype(BF)

    class GatherGram:
        def __init__(self, s0, s1):
            self.s0, self.s1 = s0, s1

        def at(self, off, t):
            return g.at[self.s0 : self.s1, rows(off + t * H, H)]

        def own(self, t):
            send(f"g_r{self.s0}{t}", self.at(q0, t), self.at(q0, t), "yr")
            send(f"g_l{self.s0}{t}", self.at(q0, t), self.at(q0, t), "yl")

        def near(self, t):
            recv(f"g_r{self.s0}{t}", self.at(ql, t))
            recv(f"g_l{self.s0}{t}", self.at(qr, t))
            if t == 0:
                send(f"g_rr{self.s0}", self.at(ql, 0), self.at(ql, 0), "yr")
            else:
                send(f"g_ll{self.s0}", self.at(qr, 1), self.at(qr, 1), "yl")

        def far(self):
            recv(f"g_rr{self.s0}", self.at(q2, 0))
            recv(f"g_ll{self.s0}", self.at(q2, 1))

    def product(offs, places, s0, s1):
        for n in range(K // 256):
            cols = slice(n * 256, n * 256 + 256)
            part = None
            for s in range(s0, s1):
                lhs = jnp.concatenate([g[s, rows(off, H), :] for off in offs], axis=0)
                rhs = xc[s, :, :, :, :, :, cols].reshape(S_ROWS, 256)
                d = jnp.dot(lhs, rhs, preferred_element_type=F32)
                part = d if part is None else part + d
            for j, (off, place) in enumerate(zip(offs, places)):
                p = part[j * H : (j + 1) * H]
                if s0 > 0:
                    p += yb[rows(off, H), cols]
                if s1 < 8:
                    yb[rows(off, H), cols] = p
                else:
                    w = B * x_ref[rows(off, H), cols].astype(F32) + C * p
                    wc[(0, *place, slice(None), cols)] = w.astype(BF)

    def update(s):
        for n in range(K // 256):
            cols = slice(n * 256, n * 256 + 256)
            u = jnp.dot(g[s], wc[s, :, :, :, :, :, cols].reshape(S_ROWS, 256), preferred_element_type=F32)
            u += ua[:, cols] if s != 0 else A * x_ref[:, cols].astype(F32)
            if s != 5:
                ua[:, cols] = u
            else:
                o_ref[:, cols] = (FACTOR * u).astype(BF)

    hi, lo = y // 2, y % 2
    gx = [Gather(f"x{c}", xc, lambda k, c=c: (c, k)) for c in range(2)]
    gw = [
        Gather("w0", wc, lambda k: (hi, k, lo)),
        Gather("w1", wc, lambda k: (slice(None), k, 1 - lo, 0)),
        Gather("w2", wc, lambda k: (slice(None), k, 1 - lo, 1)),
        Gather("w3", wc, lambda k: (1 - hi, k, lo)),
    ]
    even, odd = (1 - lo) * Q, (3 - lo) * Q
    w0 = ([q0, q0 + H], [(hi, core, lo, 0), (hi, core, lo, 1)])
    w1 = ([even, odd], [(0, core, 1 - lo, 0), (1, core, 1 - lo, 0)])
    w2 = ([even + H, odd + H], [(0, core, 1 - lo, 1), (1, core, 1 - lo, 1)])
    w3 = ([q2, q2 + H], [(1 - hi, core, lo, 0), (1 - hi, core, lo, 1)])
    gg = [GatherGram(s0, s1) for s0, s1 in GROUPS]

    def each(f, units):
        for u in units:
            f(*u)

    def end(s):
        for part in gw:
            part.from_sib(s)
        update(s)

    gx[0].own()
    gx[1].own()
    each(begin, [(0, 0), (0, 1)])
    gx[0].near()
    each(rs2, [(0, 1)])
    each(begin, [(1, 0)])
    each(rs2, [(0, 0)])
    each(begin, [(2, 0)])
    each(rs3, [(0, 1)])
    each(rs2, [(1, 0)])
    gx[0].near_z()
    each(begin, [(3, 0)])
    gx[1].near_z()
    each(rs3, [(0, 0)])
    gx[1].near()
    gx[0].pass_z()
    each(rs2, [(2, 0)])
    each(rs3, [(1, 0)])
    each(rs2, [(3, 0)])
    gx[0].far()
    each(begin, [(1, 1), (3, 1), (2, 1)])
    gx[1].pass_z()
    each(begin, [(4, 0)])
    each(rs2, [(1, 1)])
    each(rs4, [(0, 1)])
    each(rs2, [(3, 1)])
    gx[1].far()
    each(begin, [(4, 1)])
    each(rs2, [(2, 1), (4, 0), (4, 1)])
    gx[0].far_z()
    gx[0].mid()
    each(begin, [(5, 0), (6, 0)])
    each(rs3, [(1, 1), (4, 1), (3, 1)])
    each(rs4, [(1, 0)])
    each(begin, [(7, 0)])
    each(rs2, [(5, 0), (6, 0), (7, 0)])
    gx[1].far_z()
    each(rs3, [(2, 1), (2, 0)])
    each(begin, [(5, 1)])
    each(rs4, [(4, 1)])
    each(rs3, [(3, 0)])
    each(rs4, [(1, 1), (0, 0)])
    gx[1].mid()
    each(rs3, [(4, 0)])
    gg[0].own(0)
    each(rs3, [(5, 0)])
    each(begin, [(7, 1)])
    each(rs4, [(2, 1), (3, 1)])
    each(rs3, [(7, 0)])
    product(*w0, 0, 2)
    each(begin, [(6, 1)])
    each(rs2, [(5, 1)])
    each(rs4, [(2, 0)])
    each(rs3, [(6, 0)])
    each(rs4, [(3, 0)])
    each(rs2, [(7, 1), (6, 1)])
    each(rs4, [(4, 0)])
    each(rs3, [(5, 1)])
    gg[1].own(0)
    each(rs3, [(7, 1)])
    each(rs4, [(7, 0)])
    gg[0].own(1)
    each(rs3, [(6, 1)])
    product(*w0, 2, 5)
    each(rs4, [(6, 0), (7, 1), (5, 0), (5, 1), (6, 1)])
    product(*w0, 5, 8)
    gg[2].own(0)
    gw[0].own()
    gg[1].own(1)
    gg[2].own(1)
    gg[0].near(0)
    gg[0].near(1)
    product(*w1, 0, 2)
    gw[0].near()
    gg[1].near(0)
    gg[2].near(0)
    product(*w1, 2, 8)
    gw[1].own()
    product(*w2, 0, 2)
    gg[1].near(1)
    gw[0].near_z()
    gw[0].pass_z()
    product(*w2, 2, 5)
    gw[0].far()
    gw[1].near_z()
    gg[2].near(1)
    product(*w2, 5, 8)
    gw[2].own()
    gg[0].far()
    gw[1].pass_z()
    gw[1].near()
    gw[2].near()
    gw[2].near_z()
    gw[2].pass_z()
    product(*w3, 0, 2)
    gg[1].far()
    product(*w3, 2, 5)
    gg[2].far()
    product(*w3, 5, 8)
    gw[3].own()
    gw[0].mid()
    end(0)
    gw[1].far()
    gw[3].near_z()
    gw[3].pass_z()
    gw[3].near()
    gw[0].far_z()
    end(3)
    gw[2].mid()
    end(1)
    gw[2].far()
    gw[1].mid()
    gw[1].far_z()
    end(2)
    gw[3].mid()
    end(7)
    gw[3].far()
    end(6)
    gw[2].far_z()
    gw[3].far_z()
    end(4)
    end(5)

    for copy in pending[-N_SEND:]:
        copy.wait_send()
    assert len(sites) == N_RECV, len(sites)


def shards(momentum):
    unit = (8, 2, Q, HALF)
    return pl.pallas_call(
        kernel,
        out_shape=jax.ShapeDtypeStruct((R, K), BF),
        in_specs=[pl.BlockSpec(memory_space=pl.ANY)],
        out_specs=pl.BlockSpec(memory_space=pltpu.VMEM),
        scratch_shapes=[
            pltpu.VMEM((R, K), BF),
            pltpu.VMEM(SHAPE, BF),
            pltpu.VMEM(SHAPE, BF),
            pltpu.VMEM((8, 2, R, HALF), BF),
            pltpu.VMEM((8, R, S_ROWS), BF),
            pltpu.VMEM((8, 2, H, HALF), BF),
            pltpu.VMEM((8, 2, H, HALF), BF),
            pltpu.VMEM(unit, BF),
            pltpu.VMEM(unit, BF),
            pltpu.VMEM(unit, BF),
            pltpu.VMEM((R, K), F32),
            pltpu.VMEM((R, K), F32),
            pltpu.SemaphoreType.DMA((9,)),
            pltpu.SemaphoreType.DMA((N_SEND,)),
            pltpu.SemaphoreType.DMA((N_RECV,)),
        ],
        compiler_params=pltpu.CompilerParams(
            collective_id=0, has_side_effects=True, vmem_limit_bytes=58 << 20
        ),
        cost_estimate=pl.CostEstimate(flops=15 * 10**9, bytes_accessed=2 * R * K * 2, transcendentals=0),
    )(momentum)


def solution(mesh):
    placed = (P("row", "col"),)
    return jax.shard_map(
        shards, mesh=mesh, in_specs=placed, out_specs=P("row", "col"), check_vma=False
    )
```
